32 devices in a mesh: group: 8 (over z, x), mp: 4 (over y, core).
Axes of the slice: x: 2, y: 2, z: 4, core: 2. Of those that a mesh axis runs over, the one named last changes fastest.
Arguments:
- stream: bfloat16 [4096, 3584], P('group', 'mp'), may hold values from -6 to 6
- prenorm_gain: float32 [3584], replicated, may hold values from 0.25 to 12
- query_weight: bfloat16 [3584, 4096], P(None, 'mp'), may hold values from -0.09375 to 0.09375
- key_weight: bfloat16 [3584, 2048], P(None, 'mp'), may hold values from -0.09375 to 0.09375
- value_weight: bfloat16 [3584, 2048], P(None, 'mp'), may hold values from -0.09375 to 0.09375
- output_weight: bfloat16 [4096, 3584], P('mp'), may hold values from -0.09375 to 0.09375
- adapter_down_rows: bfloat16 [32, 16, 3584], P('group', None, 'mp'), may hold values from -0.09375 to 0.09375
- adapter_up_query: bfloat16 [32, 16, 4096], P('group', None, 'mp'), may hold values from -1.5 to 1.5
- request_adapter: int32 [8, 4], replicated, may hold values from 0 to 31
- adapter_row_index: int32 [32], replicated, may hold values from 0 to 31, each once
- request_token_length: int32 [8, 4], replicated, may hold values from 1 to 256, 512 in all within a row
- continues_previous: int32 [8], replicated, may hold values from 0 to 1, as said below
- request_cache_block: int32 [8, 4], replicated, may hold values from 0 to 15, as said below
- cached_length: int32 [8, 4], replicated, may hold values from 1 to 256
- cached_rotated_keys: bfloat16 [16, 256, 2048], P('group', None, 'mp'), may hold values from -6 to 6
- cached_value_rows: bfloat16 [16, 256, 2048], P('group', None, 'mp'), may hold values from -6 to 6
Outputs:
- attn_out: bfloat16 [4096, 3584], P('group', 'mp')
The draws below stay inside these ranges and needn't reach their ends.
Inputs may be any that keep to these rules, and one draw needn't show every extreme that they name: `continues_previous`: the first group has 0; some group has 1. `request_cache_block`: the owner of block b is group b // 2; blocks may be shared by requests.
All inputs are finite; a program needn't handle non-finite values.
Results may differ from the reference program's by a relative error of at most 0.017.
The reference program's roundings to bfloat16 on the way count: a program that leaves them out, or rounds other values in their place, can miss the bound.
Values may be sent and summed in bfloat16 or wider, within the bound.
A program may use at most 128 MiB of HBM per device.

```python
import math
import jax
import jax.numpy as jnp
import numpy as np
from jax import lax

MODEL_WIDTH = 3584
QUERY_HEADS = 16
KEY_VALUE_HEADS = 8
HEAD_WIDTH = 256
ADAPTER_RANK = 16
REQS = 4
BLOCK_POSITIONS = 256
TOK_DEV = 512
MOSTLEN = 256
NGROUPS = 8
ADAPTER_TOTAL = 32
CACHE_BLOCK_TOTAL = 16
TOKENS = 4096


def draw_prenorm_gain(key, part):
    gain = jnp.exp(jax.random.uniform(key, (MODEL_WIDTH,), jnp.float32, jnp.log(0.25), jnp.log(4.0)))
    return gain


def draw_continues_previous(key, part):
    flags = jax.random.randint(key, (NGROUPS,), 0, 2).astype(jnp.int32)
    return flags.at[0].set(0).at[1].set(1)


def draw_request_cache_block(key, part):
    blocks = jax.random.randint(key, (NGROUPS, REQS), 0, CACHE_BLOCK_TOTAL).astype(jnp.int32)
    return blocks.at[0, 0].set(0).at[NGROUPS - 1, REQS - 1].set(CACHE_BLOCK_TOTAL - 1)


def draw_cached_length(key, part):
    spans = jax.random.randint(key, (NGROUPS, REQS), 1, BLOCK_POSITIONS + 1).astype(jnp.int32)
    return spans.at[0, REQS - 1].set(BLOCK_POSITIONS)


def plant(values, key, least, largest):
    dims = values.shape
    spot = [jax.random.randint(jax.random.fold_in(key, axis), (), 0, dims[axis]) for axis in range(len(dims))]
    values = values.at[tuple(spot)].set(least)
    longest = dims.index(max(dims))
    spot[longest] = (spot[longest] + 1) % dims[longest]
    return values.at[tuple(spot)].set(largest)


def block_scale(own_key, extent, pieces, low, high):
    loudness, own = 1.0, jax.random.fold_in(own_key, 6)
    for dim, blocks in pieces:
        steps = jnp.exp(jax.random.uniform(jax.random.fold_in(own, dim), (blocks,), jnp.float32, low / len(pieces), high / len(pieces)))
        loudness = loudness * jnp.repeat(steps, extent[dim] // blocks).reshape([-1 if axis == dim else 1 for axis in range(len(extent))])
    return loudness


def profile(count, total, most, lean):
    loads = [(1 << 20) // math.isqrt(standing ** lean) + 1 for standing in range(2, count + 1)]
    spare, holding = total - most - (count - 1), [1] * (count - 1)
    while spare > 0:
        candidates = [i for i in range(count - 1) if holding[i] < most]
        pool, left = sum([loads[i] for i in candidates]), spare
        for i in candidates:
            more = min(most - holding[i], max(1, left * loads[i] // pool), spare)
            holding[i] = holding[i] + more
            spare = spare - more
    return np.array([most] + holding)


def ragged_sizes(key, amount, total, bound, slope):
    if amount == 2:
        one = jax.random.randint(key, (), max(1, total - bound), min(bound, total - 1) + 1)
        return jnp.stack([one, total - one])
    sizes = jnp.asarray(profile(amount, total, bound, slope), jnp.int32)
    couples = (amount - 1) // 2
    giver, taker = sizes[1:1 + 2 * couples:2], sizes[2:2 + 2 * couples:2]
    room = jnp.minimum(giver - 1, bound - taker)
    moved = jax.random.randint(jax.random.fold_in(key, 1), (couples,), 0, 1 << 20) % (room + 1)
    sizes = sizes.at[1:1 + 2 * couples:2].set(giver - moved).at[2:2 + 2 * couples:2].set(taker + moved)
    return sizes[jax.random.permutation(jax.random.fold_in(key, 2), amount)]


def scatter_about(stream_key, shape, scale, most, cuts=(), kind=jnp.bfloat16):
    values = jax.random.normal(stream_key, shape, jnp.float32) * scale
    if len(cuts) > 0:
        values = block_scale(stream_key, shape, cuts, -0.22, 0.18) * values
    return jnp.clip(values, min=-most, max=most).astype(kind)


def setup_inputs(seed: int = 0) -> dict:
    seeds = jax.random.split(jax.random.key(seed), 17)
    stream = scatter_about(seeds[0], (TOKENS, MODEL_WIDTH), 1.0, 6.0, ((0, 8), (1, 4)))
    prenorm_gain = draw_prenorm_gain(jax.random.fold_in(seeds[16], 71), 0)
    query_weight = scatter_about(seeds[2], (MODEL_WIDTH, QUERY_HEADS * HEAD_WIDTH), MODEL_WIDTH ** -0.5, 0.09375, ((1, 4),))
    key_weight = scatter_about(seeds[3], (MODEL_WIDTH, KEY_VALUE_HEADS * HEAD_WIDTH), MODEL_WIDTH ** -0.5, 0.09375, ((1, 4),))
    value_weight = scatter_about(seeds[4], (MODEL_WIDTH, KEY_VALUE_HEADS * HEAD_WIDTH), MODEL_WIDTH ** -0.5, 0.09375, ((1, 4),))
    output_weight = scatter_about(seeds[5], (QUERY_HEADS * HEAD_WIDTH, MODEL_WIDTH), (QUERY_HEADS * HEAD_WIDTH) ** -0.5, 0.09375, ((0, 4),))
    adapter_down_rows = scatter_about(seeds[6], (ADAPTER_TOTAL, ADAPTER_RANK, MODEL_WIDTH), MODEL_WIDTH ** -0.5, 0.09375, ((0, 8), (2, 4)))
    adapter_up_query = scatter_about(seeds[7], (ADAPTER_TOTAL, ADAPTER_RANK, QUERY_HEADS * HEAD_WIDTH), ADAPTER_RANK ** -0.5, 1.5, ((0, 8), (2, 4)))
    request_adapter = plant(jax.random.randint(seeds[8], (NGROUPS, REQS), 0, ADAPTER_TOTAL), jax.random.fold_in(seeds[8], 1), 0, ADAPTER_TOTAL - 1).astype(jnp.int32)
    adapter_row_index = jax.random.permutation(seeds[9], ADAPTER_TOTAL).astype(jnp.int32)
    request_token_length = jax.vmap(lambda own: ragged_sizes(own, REQS, TOK_DEV, MOSTLEN, 2))(jax.random.split(seeds[10], NGROUPS)).reshape((NGROUPS, REQS)).astype(jnp.int32)
    continues_previous = draw_continues_previous(jax.random.fold_in(seeds[16], 71), 0)
    request_cache_block = draw_request_cache_block(jax.random.fold_in(seeds[16], 71), 0)
    cached_length = draw_cached_length(jax.random.fold_in(seeds[16], 71), 0)
    cached_rotated_keys = scatter_about(seeds[14], (CACHE_BLOCK_TOTAL, BLOCK_POSITIONS, KEY_VALUE_HEADS * HEAD_WIDTH), 1.0, 6.0, ((0, 8), (2, 4)))
    cached_value_rows = scatter_about(seeds[15], (CACHE_BLOCK_TOTAL, BLOCK_POSITIONS, KEY_VALUE_HEADS * HEAD_WIDTH), 1.0, 6.0, ((0, 8), (2, 4)))
    return {"stream": stream, "prenorm_gain": prenorm_gain, "query_weight": query_weight, "key_weight": key_weight, "value_weight": value_weight, "output_weight": output_weight, "adapter_down_rows": adapter_down_rows, "adapter_up_query": adapter_up_query, "request_adapter": request_adapter, "adapter_row_index": adapter_row_index, "request_token_length": request_token_length, "continues_previous": continues_previous, "request_cache_block": request_cache_block, "cached_length": cached_length, "cached_rotated_keys": cached_rotated_keys, "cached_value_rows": cached_value_rows}


adapter_scale = 2.0

def rotate(values, position, head_size):
    count = values.shape[0]
    shaped = values.reshape(count, -1, head_size)
    half = head_size // 2
    freq = 10000.0 ** (-jnp.arange(half, dtype=jnp.float32) / half)
    angle = position[:, None, None] * freq[None, None, :]
    cosine = jnp.cos(angle)
    sine = jnp.sin(angle)
    first = shaped[..., :half]
    second = shaped[..., half:]
    turned = jnp.concatenate([first * cosine - second * sine, second * cosine + first * sine], axis=-1)
    return turned.reshape(count, -1)

def layout(lengths, cached, split_flag, prev_len, count):
    ends = jnp.cumsum(lengths).astype(jnp.int32)
    starts = (ends - lengths).astype(jnp.int32)
    place = jnp.arange(count, dtype=jnp.int32)
    member = ((place[:, None] >= starts[None, :]) & (place[:, None] < ends[None, :])).astype(jnp.int32)
    request = lax.optimization_barrier(jnp.sum(member * jnp.arange(lengths.shape[0], dtype=jnp.int32)[None, :], axis=1)).astype(jnp.int32)
    offset = place - lax.optimization_barrier(jnp.sum(member * starts[None, :], axis=1)).astype(jnp.int32)
    extra = jnp.where(request == 0, split_flag * prev_len, 0).astype(jnp.int32)
    position = lax.optimization_barrier(jnp.sum(member * cached[None, :], axis=1)).astype(jnp.int32) + extra + offset
    return (member, request, position.astype(jnp.float32))

def attend(query_vectors, keys, values, prev_keys, prev_values, cache_keys, cache_values, request, cached, split_flag, prev_len, head_size):
    count = query_vectors.shape[0]
    kv_heads = keys.shape[1] // head_size
    ratio = query_vectors.shape[1] // keys.shape[1]
    block = cache_keys.shape[1]
    slots = cache_keys.shape[0] * block
    every_key = jnp.concatenate([cache_keys.reshape(slots, -1), prev_keys, keys], 0).reshape(-1, kv_heads, head_size)
    every_value = jnp.concatenate([cache_values.reshape(slots, -1), prev_values, values], 0).reshape(-1, kv_heads, head_size)
    slot_req = (jnp.arange(slots, dtype=jnp.int32) // block).astype(jnp.int32)
    slot_col = (jnp.arange(slots, dtype=jnp.int32) % block).astype(jnp.int32)
    cache_ok = (request[:, None] == slot_req[None, :]) & (slot_col[None, :] < cached[slot_req][None, :])
    place = jnp.arange(count, dtype=jnp.int32)
    prev_ok = (split_flag == 1) & (request[:, None] == 0) & (place[None, :] >= count - prev_len)
    own_ok = (request[:, None] == request[None, :]) & (place[None, :] <= place[:, None])
    allowed = jnp.concatenate([cache_ok, prev_ok, own_ok], 1)
    grouped = query_vectors.reshape(count, kv_heads, ratio, head_size)
    scores = jnp.einsum('tkrd,skd->krts', grouped.astype(jnp.float32), every_key.astype(jnp.float32)) * head_size ** (-0.5)
    scores = jnp.where(allowed[None, None], scores, jnp.float32(-1e+30))
    top = lax.optimization_barrier(jnp.max(scores, axis=-1, keepdims=True))
    weights = jnp.exp(scores - top)
    total = lax.optimization_barrier(jnp.sum(weights, axis=-1))
    rounded = weights.astype(jnp.bfloat16).astype(jnp.float32)
    numer = jnp.einsum('krts,skd->tkrd', rounded, every_value.astype(jnp.float32))
    result = numer / jnp.transpose(total, (2, 0, 1))[..., None]
    return result.reshape(count, -1).astype(jnp.bfloat16)

def reference(stream, prenorm_gain, query_weight, key_weight, value_weight, output_weight, adapter_down_rows, adapter_up_query, request_adapter, adapter_row_index, request_token_length, continues_previous, request_cache_block, cached_length, cached_rotated_keys, cached_value_rows):
    wide = stream.astype(jnp.float32)
    normalized_input = (wide * lax.rsqrt(lax.optimization_barrier(jnp.mean(wide * wide, axis=1, keepdims=True)) + 1e-06) * prenorm_gain.astype(jnp.float32)).astype(jnp.bfloat16)
    prev_lens = jnp.concatenate([jnp.zeros((1,), jnp.int32), request_token_length[:-1, -1].astype(jnp.int32)])
    members, requests, positions = jax.vmap(lambda lengths, cached, flag, before: layout(lengths, cached, flag, before, TOK_DEV))(request_token_length, cached_length, continues_previous, prev_lens)
    position = positions.reshape(-1)
    ids_tok = jnp.take_along_axis(request_adapter, requests, axis=1).reshape(-1)
    rows = adapter_row_index[ids_tok]
    select = (rows[:, None] == jnp.arange(ADAPTER_TOTAL, dtype=jnp.int32)[None, :]).astype(jnp.float32)
    all_low_rank = jnp.einsum('vx,nhx->vnh', normalized_input.astype(jnp.float32), adapter_down_rows.astype(jnp.float32))
    low = lax.optimization_barrier(jnp.sum(select[:, :, None] * all_low_rank, axis=1)).astype(jnp.bfloat16)
    token_spread = select[:, :, None] * low.astype(jnp.float32)[:, None, :]
    query_update = jnp.einsum('jqz,qzs->js', token_spread, adapter_up_query.astype(jnp.float32))
    query_vectors = jnp.dot(normalized_input, query_weight, preferred_element_type=jnp.float32) + adapter_scale * query_update
    query_vectors = rotate(query_vectors, position, HEAD_WIDTH).astype(jnp.bfloat16)
    keys = rotate(jnp.dot(normalized_input, key_weight, preferred_element_type=jnp.float32), position, HEAD_WIDTH).astype(jnp.bfloat16)
    values = jnp.dot(normalized_input, value_weight, preferred_element_type=jnp.float32).astype(jnp.bfloat16)

    def one_group(index):
        before = jnp.maximum(index - 1, 0)
        start = (index * TOK_DEV).astype(jnp.int32)
        start_prev = (before * TOK_DEV).astype(jnp.int32)
        q_rows = lax.dynamic_slice_in_dim(query_vectors, start, TOK_DEV, 0)
        k_rows = lax.dynamic_slice_in_dim(keys, start, TOK_DEV, 0)
        v_rows = lax.dynamic_slice_in_dim(values, start, TOK_DEV, 0)
        k_prev = lax.dynamic_slice_in_dim(keys, start_prev, TOK_DEV, 0)
        v_prev = lax.dynamic_slice_in_dim(values, start_prev, TOK_DEV, 0)
        blocks = request_cache_block[index]
        return attend(q_rows, k_rows, v_rows, k_prev, v_prev, cached_rotated_keys[blocks], cached_value_rows[blocks], requests[index], cached_length[index], continues_previous[index], prev_lens[index], HEAD_WIDTH)
    attended = lax.map(one_group, jnp.arange(NGROUPS, dtype=jnp.int32)).reshape(TOKENS, -1)
    return jnp.dot(attended, output_weight, preferred_element_type=jnp.float32).astype(jnp.bfloat16)
```

```python
import functools

import jax
import jax.numpy as jnp
from jax import lax
from jax.experimental import pallas as pl
from jax.experimental.pallas import tpu as pltpu
from jax.sharding import PartitionSpec as P

HEAD_WIDTH = 256
REQS = 4
ADAPTER_SCALE = 2.0
MESH = pl.DeviceIdType.MESH
F32 = jnp.float32
BF16 = jnp.bfloat16


def dot(a, b):
    return jnp.dot(a, b, preferred_element_type=F32)


def layout(lengths, cached, extra0, count):
    ends = jnp.cumsum(lengths)
    starts = ends - lengths
    place = jnp.arange(count, dtype=jnp.int32)
    member = (place[:, None] >= starts[None, :]) & (place[:, None] < ends[None, :])
    shift = cached - starts + jnp.where(jnp.arange(REQS) == 0, extra0, 0)
    position = place + jnp.sum(jnp.where(member, shift[None, :], 0), axis=1)
    return member, position.astype(F32)


def gather_kernel(
    G, M,
    ids, stream, gain, cosine, sine, own_columns, wq_in, wk_in, wv_in, down_in, up_in, ck_in, cv_in,
    q_out, k_out, v_out, pk_out, pv_out, gk, gv,
    parts, normed, wq, wk, wv, gd, gu, cd,
    local_sem, st_send, st_recv, fw_send, fw_recv, ring_send, ring_recv, cd_send, cd_recv,
    sh_send, sh_recv,
):
    g = lax.axis_index("group")
    m = lax.axis_index("mp")
    Y = M // 2
    half = G // 2
    y, c = m // 2, m % 2
    count = stream.shape[0]
    piece = count // 2
    width = stream.shape[1]
    partner = y * 2 + 1 - c

    def group_of(p):
        p = lax.rem(p + G, G)
        x = p // half
        z = p + x * (G - 1 - 2 * p)
        return 2 * z + x

    z, x = g // 2, g % 2
    place = z + x * (G - 1 - 2 * z)
    right, left = group_of(place + 1), group_of(place - 1)
    following, before = lax.rem(g + 1, G), lax.rem(g + G - 1, G)

    local = []
    for i, (src, dst) in enumerate(
        [(wk_in, wk), (wv_in, wv), (wq_in, wq), (down_in, gd.at[g]), (up_in, gu.at[g]),
         (ck_in, gk.at[g]), (cv_in, gv.at[g])]
    ):
        local.append(pltpu.make_async_copy(src, dst, local_sem.at[i]))
        local[-1].start()

    barrier = pltpu.get_barrier_semaphore()
    for d in range(1, M):
        pl.semaphore_signal(barrier, inc=1, device_id=(g, lax.rem(m + d, M)), device_id_type=MESH)
    for other in (right, left, following, before):
        pl.semaphore_signal(barrier, inc=1, device_id=(other, m), device_id_type=MESH)
    pl.semaphore_wait(barrier, M + 3)

    def rows_of(r):
        return pl.ds(r * piece, piece)

    def stream_send(d, r):
        to = partner if d == 0 else lax.rem(y + d, Y) * 2 + c
        return pltpu.make_async_remote_copy(
            src_ref=stream.at[rows_of(r)], dst_ref=parts.at[m, rows_of(r)],
            send_sem=st_send.at[d, r], recv_sem=st_recv.at[d, r],
            device_id=(g, to), device_id_type=MESH)

    def stream_got(d, r):
        owner = partner if d == 0 else lax.rem(y - d + Y, Y) * 2 + c
        return pltpu.make_async_remote_copy(
            src_ref=stream.at[rows_of(r)], dst_ref=parts.at[owner, rows_of(r)],
            send_sem=st_send.at[d, r], recv_sem=st_recv.at[d, r],
            device_id=(g, partner), device_id_type=MESH)

    def forward(d, r):
        owner = lax.rem(y - d + Y, Y) * 2 + c
        return pltpu.make_async_remote_copy(
            src_ref=parts.at[owner, rows_of(r)], dst_ref=parts.at[owner, rows_of(r)],
            send_sem=fw_send.at[d - 1, r], recv_sem=fw_recv.at[d - 1, r],
            device_id=(g, partner), device_id_type=MESH)

    def forwarded(d, r):
        owner = lax.rem(y - d + Y, Y) * 2 + 1 - c
        return pltpu.make_async_remote_copy(
            src_ref=parts.at[owner, rows_of(r)], dst_ref=parts.at[owner, rows_of(r)],
            send_sem=fw_send.at[d - 1, r], recv_sem=fw_recv.at[d - 1, r],
            device_id=(g, partner), device_id_type=MESH)

    held = (gd, gu, gk, gv)
    own = (down_in, up_in, ck_in, cv_in)

    def ring(a, way, s):
        sign = 1 if way == 0 else -1
        owner = group_of(place - sign * (s - 1))
        return pltpu.make_async_remote_copy(
            src_ref=own[a] if s == 1 else held[a].at[owner], dst_ref=held[a].at[owner],
            send_sem=ring_send.at[a, way, s - 1], recv_sem=ring_recv.at[a, way, s - 1],
            device_id=(right if way == 0 else left, m), device_id_type=MESH)

    def ring_got(a, way, s):
        sign = 1 if way == 0 else -1
        owner = group_of(place - sign * s)
        return pltpu.make_async_remote_copy(
            src_ref=own[a], dst_ref=held[a].at[owner],
            send_sem=ring_send.at[a, way, s - 1], recv_sem=ring_recv.at[a, way, s - 1],
            device_id=(right if way == 0 else left, m), device_id_type=MESH)

    def travels(a, way, s):
        return s < half or (s == half and a % 2 == way)

    def launch(arrays, s):
        for a in arrays:
            for way in range(2):
                if travels(a, way, s):
                    ring(a, way, s).start()

    def advance(arrays, s):
        for a in arrays:
            for way in range(2):
                if travels(a, way, s):
                    ring_got(a, way, s).wait_recv()
                if travels(a, way, s + 1):
                    ring(a, way, s + 1).start()

    order = (1, 0)
    launch((0, 1), 1)
    for r in order:
        for d in range(1, Y):
            stream_send(d, r).start()
        stream_send(0, r).start()
    parts[m] = stream[...]
    advance((0, 1), 1)
    launch((2, 3), 1)
    for s in range(2, half + 1):
        advance((0, 1), s)

    def norm(r):
        rows = rows_of(r)
        for d in range(1, Y):
            stream_got(d, r).wait_recv()
            forward(d, r).start()
        stream_got(0, r).wait_recv()
        for d in range(1, Y):
            forwarded(d, r).wait_recv()
        square = jnp.zeros((piece, 1), F32)
        for p in range(M):
            wide = parts[p, rows].astype(F32)
            square = square + jnp.sum(wide * wide, axis=1, keepdims=True)
        scale = lax.rsqrt(square / (M * width) + 1e-06)
        for p in range(M):
            normed[p, rows] = (parts[p, rows].astype(F32) * scale * gain[p]).astype(BF16)

    def project(r, weight, out, turn, low=None):
        rows = rows_of(r)

        @pl.loop(0, out.shape[1] // HEAD_WIDTH)
        def _(h):
            cols = pl.ds(pl.multiple_of(h * HEAD_WIDTH, HEAD_WIDTH), HEAD_WIDTH)
            total = dot(normed[0, rows], weight[0, :, cols])
            for p in range(1, M):
                total = total + dot(normed[p, rows], weight[p, :, cols])
            if low is not None:
                up = jnp.concatenate(
                    [gu[ids[i] // per, lax.rem(ids[i], per), :, cols] for i in range(REQS)], axis=0)
                total = total + ADAPTER_SCALE * dot(low, up)
            if turn:
                first, second = total[:, : HEAD_WIDTH // 2], total[:, HEAD_WIDTH // 2:]
                cs, sn = cosine[rows], sine[rows]
                total = jnp.concatenate(
                    [first * cs - second * sn, second * cs + first * sn], axis=1)
            out[rows, cols] = total.astype(BF16)

    per = gd.shape[1]
    last = pl.ds(count - piece, piece)

    def shift(i):
        src, dst = ((k_out, pk_out), (v_out, pv_out))[i]
        return pltpu.make_async_remote_copy(
            src_ref=src.at[last], dst_ref=dst, send_sem=sh_send.at[i], recv_sem=sh_recv.at[i],
            device_id=(following, m), device_id_type=MESH)

    local[3].wait()
    local[4].wait()
    for i in range(REQS):
        cd[m, i] = gd[ids[i] // per, lax.rem(ids[i], per)]

    def chosen(d):
        return pltpu.make_async_remote_copy(
            src_ref=cd.at[m], dst_ref=cd.at[m], send_sem=cd_send.at[d - 1],
            recv_sem=cd_recv.at[d - 1], device_id=(g, lax.rem(m + d, M)), device_id_type=MESH)

    def chosen_got(d):
        return pltpu.make_async_remote_copy(
            src_ref=cd.at[m], dst_ref=cd.at[lax.rem(m - d + M, M)], send_sem=cd_send.at[d - 1],
            recv_sem=cd_recv.at[d - 1], device_id=(g, lax.rem(m + d, M)), device_id_type=MESH)

    for d in range(1, M):
        chosen(d).start()

    norm(1)
    local[0].wait()
    project(1, wk, k_out, True)
    local[1].wait()
    project(1, wv, v_out, False)

    @pl.when(g < G - 1)
    def _():
        shift(0).start()
        shift(1).start()

    advance((2, 3), 1)
    norm(0)
    project(0, wk, k_out, True)
    project(0, wv, v_out, False)

    for d in range(1, M):
        chosen_got(d).wait_recv()
    local[2].wait()
    for r in order:
        low = jnp.zeros((piece, REQS * cd.shape[2]), F32)
        for p in range(M):
            factors = cd[p].reshape(REQS * cd.shape[2], width)
            low = low + lax.dot_general(
                normed[p, rows_of(r)], factors, (((1,), (1,)), ((), ())),
                preferred_element_type=F32)
        low = low.astype(BF16) * own_columns[rows_of(r)]
        project(r, wq, q_out, True, low)

    for s in range(2, half + 1):
        advance((2, 3), s)

    @pl.when(g > 0)
    def _():
        shift(0).wait_recv()
        shift(1).wait_recv()

    @pl.when(g == 0)
    def _():
        fill = [pltpu.make_async_copy(a.at[last], b, sh_recv.at[i])
                for i, (a, b) in enumerate(((k_out, pk_out), (v_out, pv_out)))]
        for one in fill:
            one.start()
        for one in fill:
            one.wait()

    @pl.when(g < G - 1)
    def _():
        shift(0).wait_send()
        shift(1).wait_send()

    for r in order:
        for d in range(Y):
            stream_send(d, r).wait_send()
        for d in range(1, Y):
            forward(d, r).wait_send()
    for a in range(4):
        for way in range(2):
            for s in range(1, half + 1):
                if travels(a, way, s):
                    ring(a, way, s).wait_send()
    for d in range(1, M):
        chosen(d).wait_send()
    local[5].wait()
    local[6].wait()


def attend_kernel(info, q, k, v, pk, pv, *rest):
    cache_k, cache_v, out = rest[:REQS], rest[REQS:2 * REQS], rest[2 * REQS]
    count = q.shape[0]
    tile = min(128, count)
    block = cache_k[0].shape[1]
    piece = pk.shape[0]
    ratio = q.shape[1] // HEAD_WIDTH
    starts, ends, cached = [], [], []
    run = jnp.int32(0)
    for r in range(REQS):
        starts.append(run)
        run = run + info[REQS + r]
        ends.append(run)
        cached.append(info[2 * REQS + r])
    flag, prev_len = info[3 * REQS], info[3 * REQS + 1]
    cut = jnp.where(flag == 1, piece - prev_len, piece)
    turned = (((1,), (1,)), ((), ()))
    for t in range(count // tile):
        rows = pl.ds(t * tile, tile)
        seen = (t + 1) * tile
        place = t * tile + lax.broadcasted_iota(jnp.int32, (tile, 1), 0)
        begin = jnp.zeros((tile, 1), jnp.int32)
        limit = []
        for r in range(REQS):
            mine = (place >= starts[r]) & (place < ends[r])
            begin = jnp.where(mine, starts[r], begin)
            limit.append(jnp.where(mine, cached[r], 0))
        from_prev = jnp.where(place < ends[0], cut, piece)
        col = lax.broadcasted_iota(jnp.int32, (tile, block), 1)
        col_prev = lax.broadcasted_iota(jnp.int32, (tile, piece), 1)
        col_own = lax.broadcasted_iota(jnp.int32, (tile, seen), 1)
        masks = [col < limit[r] for r in range(REQS)]
        masks.append(col_prev >= from_prev)
        masks.append((col_own >= begin) & (col_own <= place))
        keys = [cache_k[r][0] for r in range(REQS)] + [pk[...], k[:seen]]
        values = [cache_v[r][0] for r in range(REQS)] + [pv[...], v[:seen]]
        for h in range(ratio):
            cols = pl.ds(h * HEAD_WIDTH, HEAD_WIDTH)
            query = q[rows, cols]
            scores = [
                jnp.where(ok, lax.dot_general(query, key, turned, preferred_element_type=F32)
                          * HEAD_WIDTH ** -0.5, -1e30)
                for key, ok in zip(keys, masks)
            ]
            top = jnp.max(scores[0], axis=1, keepdims=True)
            for one in scores[1:]:
                top = jnp.maximum(top, jnp.max(one, axis=1, keepdims=True))
            total = jnp.zeros((tile, 1), F32)
            numer = jnp.zeros((tile, HEAD_WIDTH), F32)
            for one, value in zip(scores, values):
                weight = jnp.exp(one - top)
                total = total + jnp.sum(weight, axis=1, keepdims=True)
                numer = numer + dot(weight.astype(BF16), value)
            out[rows, cols] = (numer / total).astype(BF16)


def output_kernel(
    M, sliced, att, wo_in, out,
    wo, hold, mail, partner_in, post, post_in, own,
    local_sem, p_send, p_recv, y_send, y_recv,
):
    g = lax.axis_index("group")
    m = lax.axis_index("mp")
    Y = M // 2
    y, c = m // 2, m % 2
    partner = y * 2 + 1 - c
    width = out.shape[1]
    pieces = 2
    piece = out.shape[0] // pieces
    targets = [lax.rem(y + d, Y) * 2 + (c if e == 0 else 1 - c) for d in range(Y) for e in range(2)]
    loads = []
    for i, to in enumerate(targets):
        if sliced:
            src = wo_in.at[:, pl.ds(pl.multiple_of(to * width, 128), width)]
        else:
            src = wo_in.at[to]
        loads.append(pltpu.make_async_copy(src, wo.at[i], local_sem.at[i]))
    turn = [2 * d + e for d in list(range(1, Y)) + [0] for e in (1, 0)]
    for i in turn:
        loads[i].start()

    barrier = pltpu.get_barrier_semaphore()
    pl.semaphore_signal(barrier, inc=1, device_id=(g, partner), device_id_type=MESH)
    for d in range(1, Y):
        pl.semaphore_signal(
            barrier, inc=1, device_id=(g, lax.rem(y + d, Y) * 2 + c), device_id_type=MESH)
    pl.semaphore_wait(barrier, Y)

    def share(i, r):
        return dot(att[pl.ds(r * piece, piece)], wo[i])

    def to_partner(d, r):
        return pltpu.make_async_remote_copy(
            src_ref=mail.at[d, r], dst_ref=partner_in.at[d, r], send_sem=p_send.at[d, r],
            recv_sem=p_recv.at[d, r], device_id=(g, partner), device_id_type=MESH)

    def along(d, r):
        return pltpu.make_async_remote_copy(
            src_ref=post.at[d - 1, r], dst_ref=post_in.at[d - 1, r], send_sem=y_send.at[d - 1, r],
            recv_sem=y_recv.at[d - 1, r], device_id=(g, lax.rem(y + d, Y) * 2 + c),
            device_id_type=MESH)

    def give(d, r):
        mail[d, r] = share(2 * d + 1, r).astype(BF16)
        to_partner(d, r).start()

    def combine(d, r):
        to_partner(d, r).wait_recv()
        post[d - 1, r] = (hold[r] + partner_in[d, r].astype(F32)).astype(BF16)
        along(d, r).start()

    for d in range(1, Y):
        loads[2 * d + 1].wait()
        give(d, 0)
        loads[2 * d].wait()
        hold[0] = share(2 * d, 0)
        give(d, 1)
        combine(d, 0)
        hold[1] = share(2 * d, 1)
        combine(d, 1)
    loads[1].wait()
    give(0, 0)
    give(0, 1)
    loads[0].wait()
    for r in range(pieces):
        own[r] = share(0, r)
    for r in range(pieces):
        to_partner(0, r).wait_recv()
        total = own[r] + partner_in[0, r].astype(F32)
        for d in range(1, Y):
            along(d, r).wait_recv()
            total = total + post_in[d - 1, r].astype(F32)
        out[pl.ds(r * piece, piece)] = total.astype(BF16)
    for r in range(pieces):
        for d in range(Y):
            to_partner(d, r).wait_send()
        for d in range(1, Y):
            along(d, r).wait_send()


def on_device(
    G, M,
    stream, prenorm_gain, query_weight, key_weight, value_weight, output_weight,
    adapter_down_rows, adapter_up_query, request_adapter, adapter_row_index,
    request_token_length, continues_previous, request_cache_block, cached_length,
    cached_rotated_keys, cached_value_rows,
):
    count, width = stream.shape
    nq, nk = query_weight.shape[1], key_weight.shape[1]
    Y, half, piece = M // 2, G // 2, count // 2
    per, rank = adapter_down_rows.shape[:2]
    owned, block = cached_rotated_keys.shape[:2]
    group_at = lax.axis_index("group")
    before = jnp.maximum(group_at - 1, 0)
    lengths = request_token_length[group_at]
    cached = cached_length[group_at]
    flag = continues_previous[group_at]
    prev_len = request_token_length[before, REQS - 1]
    member, position = layout(lengths, cached, flag * prev_len, count)
    freq = 10000.0 ** (-jnp.arange(HEAD_WIDTH // 2, dtype=F32) / (HEAD_WIDTH // 2))
    angle = position[:, None] * freq[None, :]
    own_columns = jnp.repeat(member, rank, axis=1).astype(BF16)
    ids = adapter_row_index[request_adapter[group_at]]

    vmem, anywhere = pl.BlockSpec(memory_space=pltpu.VMEM), pl.BlockSpec(memory_space=pl.ANY)
    dma = pltpu.SemaphoreType.DMA
    flops = 2 * count * width * M * (nq + 2 * nk)
    q, k, v, pk, pv, gk, gv = pl.pallas_call(
        functools.partial(gather_kernel, G, M),
        out_shape=[
            jax.ShapeDtypeStruct((count, nq), BF16),
            jax.ShapeDtypeStruct((count, nk), BF16),
            jax.ShapeDtypeStruct((count, nk), BF16),
            jax.ShapeDtypeStruct((piece, nk), BF16),
            jax.ShapeDtypeStruct((piece, nk), BF16),
            jax.ShapeDtypeStruct((G, owned, block, nk), BF16),
            jax.ShapeDtypeStruct((G, owned, block, nk), BF16),
        ],
        in_specs=[pl.BlockSpec(memory_space=pltpu.SMEM)] + [vmem] * 5 + [anywhere] * 7,
        out_specs=[vmem] * 3 + [anywhere] * 4,
        scratch_shapes=[
            pltpu.VMEM((M, count, width), BF16),
            pltpu.VMEM((M, count, width), BF16),
            pltpu.VMEM((M, width, nq), BF16),
            pltpu.VMEM((M, width, nk), BF16),
            pltpu.VMEM((M, width, nk), BF16),
            pltpu.VMEM((G, per, rank, width), BF16),
            pltpu.VMEM((G, per, rank, nq), BF16),
            pltpu.VMEM((M, REQS, rank, width), BF16),
            dma((7,)), dma((Y, 2)), dma((Y, 2)), dma((Y - 1, 2)), dma((Y - 1, 2)),
            dma((4, 2, half)), dma((4, 2, half)), dma((M - 1,)), dma((M - 1,)), dma((2,)), dma((2,)),
        ],
        compiler_params=pltpu.CompilerParams(
            collective_id=0, has_side_effects=True, vmem_limit_bytes=48 * 2 ** 20),
        cost_estimate=pl.CostEstimate(flops=flops, bytes_accessed=32 * 2 ** 20, transcendentals=0),
        name="gather_project",
    )(
        ids, stream, prenorm_gain.reshape(M, 1, width), jnp.cos(angle), jnp.sin(angle), own_columns,
        query_weight.reshape(M, width, nq), key_weight.reshape(M, width, nk),
        value_weight.reshape(M, width, nk), adapter_down_rows, adapter_up_query,
        cached_rotated_keys, cached_value_rows,
    )

    info = jnp.concatenate(
        [request_cache_block[group_at], lengths, cached, flag[None], prev_len[None]])
    heads = nk // HEAD_WIDTH
    each = nq // heads

    def head(h, info):
        return (0, h)

    def picked(r):
        return pl.BlockSpec((1, block, HEAD_WIDTH), lambda h, info: (info[r], 0, h))

    blocks = [picked(r) for r in range(REQS)]
    own_kv = pl.BlockSpec((count, HEAD_WIDTH), head)
    prev_kv = pl.BlockSpec((piece, HEAD_WIDTH), head)
    every_k = gk.reshape(G * owned, block, nk)
    every_v = gv.reshape(G * owned, block, nk)
    attended = pl.pallas_call(
        attend_kernel,
        out_shape=jax.ShapeDtypeStruct((count, nq), BF16),
        grid_spec=pltpu.PrefetchScalarGridSpec(
            num_scalar_prefetch=1,
            grid=(heads,),
            in_specs=[pl.BlockSpec((count, each), head), own_kv, own_kv, prev_kv, prev_kv]
            + blocks + blocks,
            out_specs=pl.BlockSpec((count, each), head),
        ),
        compiler_params=pltpu.CompilerParams(vmem_limit_bytes=40 * 2 ** 20),
        name="attend",
    )(info, q, k, v, pk, pv, *([every_k] * REQS), *([every_v] * REQS))

    sliced = width % 128 == 0
    wo = output_weight
    if not sliced:
        wo = output_weight.reshape(nq, M, width).transpose(1, 0, 2)
    return pl.pallas_call(
        functools.partial(output_kernel, M, sliced),
        out_shape=jax.ShapeDtypeStruct((count, width), BF16),
        in_specs=[vmem, anywhere],
        out_specs=vmem,
        scratch_shapes=[
            pltpu.VMEM((M, nq, width), BF16),
            pltpu.VMEM((2, piece, width), F32),
            pltpu.VMEM((Y, 2, piece, width), BF16),
            pltpu.VMEM((Y, 2, piece, width), BF16),
            pltpu.VMEM((Y - 1, 2, piece, width), BF16),
            pltpu.VMEM((Y - 1, 2, piece, width), BF16),
            pltpu.VMEM((2, piece, width), F32),
            dma((M,)), dma((Y, 2)), dma((Y, 2)), dma((Y - 1, 2)), dma((Y - 1, 2)),
        ],
        compiler_params=pltpu.CompilerParams(
            collective_id=1, has_side_effects=True, vmem_limit_bytes=40 * 2 ** 20),
        name="project_out",
    )(attended, wo)


def solution(mesh):
    placed = (
        P("group", "mp"), P(), P(None, "mp"), P(None, "mp"), P(None, "mp"), P("mp", None),
        P("group", None, "mp"), P("group", None, "mp"), P(), P(), P(), P(), P(), P(),
        P("group", None, "mp"), P("group", None, "mp"),
    )
    return jax.shard_map(
        functools.partial(on_device, mesh.shape["group"], mesh.shape["mp"]),
        mesh=mesh, in_specs=placed, out_specs=P("group", "mp"), check_vma=False,
    )
```

```python
import functools

import jax
import jax.numpy as jnp
from jax import lax
from jax.experimental import pallas as pl
from jax.experimental.pallas import tpu as pltpu
from jax.sharding import PartitionSpec as P

HEAD_WIDTH = 256
REQS = 4
ADAPTER_SCALE = 2.0
MESH = pl.DeviceIdType.MESH
F32 = jnp.float32
BF16 = jnp.bfloat16


def dot(a, b):
    return jnp.dot(a, b, preferred_element_type=F32)


def layer_kernel(
    G, M, sliced,
    req_adapter, row_index, req_length, continues, req_block, req_cached,
    stream, gain, freq, wq_in, wk_in, wv_in, wo_in, down_in, up_in, ck_in, cv_in,
    out,
    q_out, k_out, v_out, pk_out, pv_out, gk, gv, cosine, sine, own_columns,
    parts, normed, wq, wk, wv, gd, gu, cd,
    acc, top, total_of, att, wo, hold, mail, partner_in, post, post_in, own_sum,
    local_sem, st_send, st_recv, fw_send, fw_recv, ring_send, ring_recv, cd_send, cd_recv,
    sh_send, sh_recv, wo_sem, p_send, p_recv, y_send, y_recv,
):
    g = lax.axis_index("group")
    m = lax.axis_index("mp")
    Y = M // 2
    half = G // 2
    y, c = m // 2, m % 2
    count = stream.shape[0]
    piece = count // 2
    width = stream.shape[1]
    partner = y * 2 + 1 - c

    def group_of(p):
        p = lax.rem(p + G, G)
        x = p // half
        z = p + x * (G - 1 - 2 * p)
        return 2 * z + x

    z, x = g // 2, g % 2
    place_in_ring = z + x * (G - 1 - 2 * z)
    right, left = group_of(place_in_ring + 1), group_of(place_in_ring - 1)
    following, before = lax.rem(g + 1, G), lax.rem(g + G - 1, G)

    local = []
    for i, (src, dst) in enumerate(
        [(wk_in, wk), (wv_in, wv), (wq_in, wq), (down_in, gd.at[g]), (up_in, gu.at[g]),
         (ck_in, gk.at[g]), (cv_in, gv.at[g])]
    ):
        local.append(pltpu.make_async_copy(src, dst, local_sem.at[i]))
        local[-1].start()
    targets = [lax.rem(y + d, Y) * 2 + (c if e == 0 else 1 - c) for d in range(Y) for e in range(2)]
    loads = []
    for i, to in enumerate(targets):
        if sliced:
            src = wo_in.at[:, pl.ds(pl.multiple_of(to * width, 128), width)]
        else:
            src = wo_in.at[to]
        loads.append(pltpu.make_async_copy(src, wo.at[i], wo_sem.at[i]))

    barrier = pltpu.get_barrier_semaphore()
    for d in range(1, M):
        pl.semaphore_signal(barrier, inc=1, device_id=(g, lax.rem(m + d, M)), device_id_type=MESH)
    for other in (right, left, following, before):
        pl.semaphore_signal(barrier, inc=1, device_id=(other, m), device_id_type=MESH)
    pl.semaphore_wait(barrier, M + 3)

    def rows_of(r):
        return pl.ds(r * piece, piece)

    def stream_send(d, r):
        to = partner if d == 0 else lax.rem(y + d, Y) * 2 + c
        return pltpu.make_async_remote_copy(
            src_ref=stream.at[rows_of(r)], dst_ref=parts.at[m, rows_of(r)],
            send_sem=st_send.at[d, r], recv_sem=st_recv.at[d, r],
            device_id=(g, to), device_id_type=MESH)

    def stream_got(d, r):
        owner = partner if d == 0 else lax.rem(y - d + Y, Y) * 2 + c
        return pltpu.make_async_remote_copy(
            src_ref=stream.at[rows_of(r)], dst_ref=parts.at[owner, rows_of(r)],
            send_sem=st_send.at[d, r], recv_sem=st_recv.at[d, r],
            device_id=(g, partner), device_id_type=MESH)

    def forward(d, r):
        owner = lax.rem(y - d + Y, Y) * 2 + c
        return pltpu.make_async_remote_copy(
            src_ref=parts.at[owner, rows_of(r)], dst_ref=parts.at[owner, rows_of(r)],
            send_sem=fw_send.at[d - 1, r], recv_sem=fw_recv.at[d - 1, r],
            device_id=(g, partner), device_id_type=MESH)

    def forwarded(d, r):
        owner = lax.rem(y - d + Y, Y) * 2 + 1 - c
        return pltpu.make_async_remote_copy(
            src_ref=parts.at[owner, rows_of(r)], dst_ref=parts.at[owner, rows_of(r)],
            send_sem=fw_send.at[d - 1, r], recv_sem=fw_recv.at[d - 1, r],
            device_id=(g, partner), device_id_type=MESH)

    held = (gd, gu, gk, gv)
    own = (down_in, up_in, ck_in, cv_in)

    def ring(a, way, s):
        sign = 1 if way == 0 else -1
        owner = group_of(place_in_ring - sign * (s - 1))
        return pltpu.make_async_remote_copy(
            src_ref=own[a] if s == 1 else held[a].at[owner], dst_ref=held[a].at[owner],
            send_sem=ring_send.at[a, way, s - 1], recv_sem=ring_recv.at[a, way, s - 1],
            device_id=(right if way == 0 else left, m), device_id_type=MESH)

    def ring_got(a, way, s):
        sign = 1 if way == 0 else -1
        owner = group_of(place_in_ring - sign * s)
        return pltpu.make_async_remote_copy(
            src_ref=own[a], dst_ref=held[a].at[owner],
            send_sem=ring_send.at[a, way, s - 1], recv_sem=ring_recv.at[a, way, s - 1],
            device_id=(right if way == 0 else left, m), device_id_type=MESH)

    def travels(a, way, s):
        return s < half or (s == half and a % 2 == way)

    def launch(arrays, s):
        for a in arrays:
            for way in range(2):
                if travels(a, way, s):
                    ring(a, way, s).start()

    def advance(arrays, s):
        for a in arrays:
            for way in range(2):
                if travels(a, way, s):
                    ring_got(a, way, s).wait_recv()
                if travels(a, way, s + 1):
                    ring(a, way, s + 1).start()

    order = (1, 0)
    launch((0, 1), 1)
    for r in order:
        for d in range(1, Y):
            stream_send(d, r).start()
        stream_send(0, r).start()
    launch((2,), 1)
    parts[m] = stream[...]
    for one in loads:
        one.start()

    lengths = [req_length[g, i] for i in range(REQS)]
    prev_len = req_length[jnp.maximum(g - 1, 0), REQS - 1]
    extra = jnp.where(continues[g] == 1, prev_len, 0)
    starts, ends = [], []
    run = jnp.int32(0)
    for i in range(REQS):
        starts.append(run)
        run = run + lengths[i]
        ends.append(run)

    def spread(rows, count, values, other):
        place = rows + lax.broadcasted_iota(jnp.int32, (count, 1), 0)
        result = jnp.full((count, 1), other, jnp.int32)
        for i in range(REQS):
            result = jnp.where((place >= starts[i]) & (place < ends[i]), values[i], result)
        return place, result

    cached = [req_cached[g, i] for i in range(REQS)]
    blocks = [req_block[g, i] for i in range(REQS)]
    ids = [row_index[req_adapter[g, i]] for i in range(REQS)]
    offsets = [cached[i] - starts[i] + (extra if i == 0 else 0) for i in range(REQS)]
    place, moved = spread(0, count, offsets, 0)
    angle = (place + moved).astype(F32) * freq[...]
    cosine[...] = jnp.cos(angle)
    sine[...] = jnp.sin(angle)
    rank = gd.shape[2]
    column = lax.broadcasted_iota(jnp.int32, (count, REQS * rank), 1)
    belongs = jnp.zeros((count, REQS * rank), F32)
    for i in range(REQS):
        mine = (place >= starts[i]) & (place < ends[i])
        mine = mine & (column >= i * rank) & (column < (i + 1) * rank)
        belongs = jnp.where(mine, 1.0, belongs)
    own_columns[...] = belongs.astype(BF16)

    advance((0, 1), 1)
    launch((3,), 1)

    def norm(r):
        rows = rows_of(r)
        for d in range(1, Y):
            stream_got(d, r).wait_recv()
            forward(d, r).start()
        stream_got(0, r).wait_recv()
        for d in range(1, Y):
            forwarded(d, r).wait_recv()
        square = jnp.zeros((piece, 1), F32)
        for p in range(M):
            wide = parts[p, rows].astype(F32)
            square = square + jnp.sum(wide * wide, axis=1, keepdims=True)
        scale = lax.rsqrt(square / (M * width) + 1e-06)
        for p in range(M):
            normed[p, rows] = (parts[p, rows].astype(F32) * scale * gain[:, p * width:(p + 1) * width]).astype(BF16)

    def project(r, weight, out, turn, low=None):
        rows = rows_of(r)

        @pl.loop(0, out.shape[1] // HEAD_WIDTH)
        def _(h):
            cols = pl.ds(pl.multiple_of(h * HEAD_WIDTH, HEAD_WIDTH), HEAD_WIDTH)
            total = dot(normed[0, rows], weight[0, :, cols])
            for p in range(1, M):
                total = total + dot(normed[p, rows], weight[p, :, cols])
            if low is not None:
                up = jnp.concatenate(
                    [gu[ids[i] // per, lax.rem(ids[i], per), :, cols] for i in range(REQS)], axis=0)
                total = total + ADAPTER_SCALE * dot(low, up)
            if turn:
                first, second = total[:, : HEAD_WIDTH // 2], total[:, HEAD_WIDTH // 2:]
                cs, sn = cosine[rows], sine[rows]
                total = jnp.concatenate(
                    [first * cs - second * sn, second * cs + first * sn], axis=1)
            out[rows, cols] = total.astype(BF16)

    per = gd.shape[1]
    last = pl.ds(count - piece, piece)

    def shift(i):
        src, dst = ((k_out, pk_out), (v_out, pv_out))[i]
        return pltpu.make_async_remote_copy(
            src_ref=src.at[last], dst_ref=dst, send_sem=sh_send.at[i], recv_sem=sh_recv.at[i],
            device_id=(following, m), device_id_type=MESH)

    def chosen(d):
        return pltpu.make_async_remote_copy(
            src_ref=cd.at[m], dst_ref=cd.at[m], send_sem=cd_send.at[d - 1],
            recv_sem=cd_recv.at[d - 1], device_id=(g, lax.rem(m + d, M)), device_id_type=MESH)

    def chosen_got(d):
        return pltpu.make_async_remote_copy(
            src_ref=cd.at[m], dst_ref=cd.at[lax.rem(m - d + M, M)], send_sem=cd_send.at[d - 1],
            recv_sem=cd_recv.at[d - 1], device_id=(g, lax.rem(m + d, M)), device_id_type=MESH)

    turned = (((1,), (1,)), ((), ()))
    heads = q_out.shape[1] // HEAD_WIDTH
    ratio = q_out.shape[1] // k_out.shape[1]

    def attend(r, keys_of, allowed, first=False):
        rows = rows_of(r)

        @pl.loop(0, heads)
        def _(h):
            cols = pl.ds(pl.multiple_of(h * HEAD_WIDTH, HEAD_WIDTH), HEAD_WIDTH)
            kv = pl.ds(pl.multiple_of(h // ratio * HEAD_WIDTH, HEAD_WIDTH), HEAD_WIDTH)
            keys, values = keys_of(kv)
            scores = lax.dot_general(
                q_out[rows, cols], keys, turned, preferred_element_type=F32) * HEAD_WIDTH ** -0.5
            scores = jnp.where(allowed, scores, -1e30)
            largest = jnp.max(scores, axis=1, keepdims=True)
            if not first:
                largest = jnp.maximum(largest, top[h, rows])
            weights = jnp.exp(scores - largest)
            total = jnp.sum(weights, axis=1, keepdims=True)
            numer = dot(weights.astype(BF16), values)
            if not first:
                fade = jnp.exp(top[h, rows] - largest)
                total = total + total_of[h, rows] * fade
                numer = numer + acc[rows, cols] * fade
            top[h, rows] = largest
            total_of[h, rows] = total
            acc[rows, cols] = numer

    def attend_own(r):
        seen = (r + 1) * piece
        at, begin = spread(r * piece, piece, starts, 0)
        col = lax.broadcasted_iota(jnp.int32, (piece, seen), 1)
        attend(r, lambda kv: (k_out[:seen, kv], v_out[:seen, kv]), (col >= begin) & (col <= at), True)

    def attend_prev(r):
        at, _ = spread(r * piece, piece, starts, 0)
        least = jnp.where(at < ends[0], piece - extra, piece)
        col = lax.broadcasted_iota(jnp.int32, (piece, piece), 1)
        attend(r, lambda kv: (pk_out[:, kv], pv_out[:, kv]), col >= least)

    owned, block = gk.shape[1], gk.shape[2]

    def attend_cache(r, owner):
        masks = []
        for i in range(owned):
            sees = [jnp.where(blocks[j] == owner * owned + i, cached[j], 0) for j in range(REQS)]
            _, limit = spread(r * piece, piece, sees, 0)
            masks.append(jnp.where(lax.broadcasted_iota(jnp.int32, (piece, block), 1) < limit, 1, 0))
        allowed = jnp.concatenate(masks, axis=1) > 0

        def keys_of(kv):
            return tuple(a[owner, :, :, kv].reshape(owned * block, HEAD_WIDTH) for a in (gk, gv))

        attend(r, keys_of, allowed)

    def finish(r):
        rows = rows_of(r)
        for h in range(heads):
            cols = pl.ds(h * HEAD_WIDTH, HEAD_WIDTH)
            att[rows, cols] = (acc[rows, cols] / total_of[h, rows]).astype(BF16)

    def share(i, r):
        return dot(att[rows_of(r)], wo[i])

    def to_partner(d, r):
        return pltpu.make_async_remote_copy(
            src_ref=mail.at[d, r], dst_ref=partner_in.at[d, r], send_sem=p_send.at[d, r],
            recv_sem=p_recv.at[d, r], device_id=(g, partner), device_id_type=MESH)

    def along(d, r):
        return pltpu.make_async_remote_copy(
            src_ref=post.at[d - 1, r], dst_ref=post_in.at[d - 1, r], send_sem=y_send.at[d - 1, r],
            recv_sem=y_recv.at[d - 1, r], device_id=(g, lax.rem(y + d, Y) * 2 + c),
            device_id_type=MESH)

    def give(d, r):
        mail[d, r] = share(2 * d + 1, r).astype(BF16)
        to_partner(d, r).start()

    def combine(d, r):
        to_partner(d, r).wait_recv()
        post[d - 1, r] = (hold[r] + partner_in[d, r].astype(F32)).astype(BF16)
        along(d, r).start()

    norm(1)
    local[0].wait()
    project(1, wk, k_out, True)
    local[1].wait()
    project(1, wv, v_out, False)

    @pl.when(g < G - 1)
    def _():
        shift(0).start()
        shift(1).start()

    advance((0, 1), 2)
    norm(0)
    project(0, wk, k_out, True)
    project(0, wv, v_out, False)
    advance((2,), 1)
    advance((0, 1), 3)
    advance((3,), 1)
    for s in range(4, half + 1):
        advance((0, 1), s)

    local[3].wait()
    local[4].wait()
    for i in range(REQS):
        cd[m, i] = gd[ids[i] // per, lax.rem(ids[i], per)]
    for d in range(1, M):
        chosen(d).start()
    for d in range(1, M):
        chosen_got(d).wait_recv()
    local[2].wait()
    for r in order:
        low = jnp.zeros((piece, REQS * rank), F32)
        for p in range(M):
            factors = cd[p].reshape(REQS * rank, width)
            low = low + lax.dot_general(
                normed[p, rows_of(r)], factors, turned, preferred_element_type=F32)
        low = low.astype(BF16) * own_columns[rows_of(r)]
        project(r, wq, q_out, True, low)

    for r in range(2):
        attend_own(r)
    advance((2, 3), 2)

    @pl.when(g > 0)
    def _():
        shift(0).wait_recv()
        shift(1).wait_recv()

    @pl.when(g == 0)
    def _():
        pk_out[...] = k_out[last]
        pv_out[...] = v_out[last]

    local[5].wait()
    local[6].wait()
    for r in range(2):
        attend_prev(r)
        attend_cache(r, g)
    for s in range(1, half):
        if s > 2:
            advance((2, 3), s)
        for sign in (-1, 1):
            for r in range(2):
                attend_cache(r, group_of(place_in_ring + sign * s))
    for one in loads:
        one.wait()
    advance((2, 3), half)
    for r in range(2):
        attend_cache(r, group_of(place_in_ring + half))
        finish(r)
        for d in range(1, Y):
            give(d, r)
            hold[r] = share(2 * d, r)
            combine(d, r)
    for r in range(2):
        give(0, r)
        own_sum[r] = share(0, r)
    for r in range(2):
        to_partner(0, r).wait_recv()
        total = own_sum[r] + partner_in[0, r].astype(F32)
        for d in range(1, Y):
            along(d, r).wait_recv()
            total = total + post_in[d - 1, r].astype(F32)
        out[rows_of(r)] = total.astype(BF16)

    @pl.when(g < G - 1)
    def _():
        shift(0).wait_send()
        shift(1).wait_send()

    for r in order:
        for d in range(Y):
            stream_send(d, r).wait_send()
            to_partner(d, r).wait_send()
        for d in range(1, Y):
            forward(d, r).wait_send()
            along(d, r).wait_send()
    for a in range(4):
        for way in range(2):
            for s in range(1, half + 1):
                if travels(a, way, s):
                    ring(a, way, s).wait_send()
    for d in range(1, M):
        chosen(d).wait_send()


def on_device(
    G, M,
    stream, prenorm_gain, query_weight, key_weight, value_weight, output_weight,
    adapter_down_rows, adapter_up_query, request_adapter, adapter_row_index,
    request_token_length, continues_previous, request_cache_block, cached_length,
    cached_rotated_keys, cached_value_rows,
):
    count, width = stream.shape
    nq, nk = query_weight.shape[1], key_weight.shape[1]
    Y, half, piece = M // 2, G // 2, count // 2
    per, rank = adapter_down_rows.shape[:2]
    owned, block = cached_rotated_keys.shape[:2]
    heads = nq // HEAD_WIDTH
    freq = 10000.0 ** (-jnp.arange(HEAD_WIDTH // 2, dtype=F32) / (HEAD_WIDTH // 2))
    sliced = width % 128 == 0
    wo = output_weight
    if not sliced:
        wo = output_weight.reshape(nq, M, width).transpose(1, 0, 2)

    smem, vmem = pl.BlockSpec(memory_space=pltpu.SMEM), pl.BlockSpec(memory_space=pltpu.VMEM)
    anywhere = pl.BlockSpec(memory_space=pl.ANY)
    dma = pltpu.SemaphoreType.DMA
    flops = 2 * count * width * M * (2 * nq + 2 * nk)
    return pl.pallas_call(
        functools.partial(layer_kernel, G, M, sliced),
        out_shape=jax.ShapeDtypeStruct((count, width), BF16),
        in_specs=[smem] * 6 + [vmem] * 3 + [anywhere] * 8,
        out_specs=vmem,
        scratch_shapes=[
            pltpu.VMEM((count, nq), BF16),
            pltpu.VMEM((count, nk), BF16),
            pltpu.VMEM((count, nk), BF16),
            pltpu.VMEM((piece, nk), BF16),
            pltpu.VMEM((piece, nk), BF16),
            pltpu.VMEM((G, owned, block, nk), BF16),
            pltpu.VMEM((G, owned, block, nk), BF16),
            pltpu.VMEM((count, HEAD_WIDTH // 2), F32),
            pltpu.VMEM((count, HEAD_WIDTH // 2), F32),
            pltpu.VMEM((count, REQS * rank), BF16),
            pltpu.VMEM((M, count, width), BF16),
            pltpu.VMEM((M, count, width), BF16),
            pltpu.VMEM((M, width, nq), BF16),
            pltpu.VMEM((M, width, nk), BF16),
            pltpu.VMEM((M, width, nk), BF16),
            pltpu.VMEM((G, per, rank, width), BF16),
            pltpu.VMEM((G, per, rank, nq), BF16),
            pltpu.VMEM((M, REQS, rank, width), BF16),
            pltpu.VMEM((count, nq), F32),
            pltpu.VMEM((heads, count, 1), F32),
            pltpu.VMEM((heads, count, 1), F32),
            pltpu.VMEM((count, nq), BF16),
            pltpu.VMEM((M, nq, width), BF16),
            pltpu.VMEM((2, piece, width), F32),
            pltpu.VMEM((Y, 2, piece, width), BF16),
            pltpu.VMEM((Y, 2, piece, width), BF16),
            pltpu.VMEM((Y - 1, 2, piece, width), BF16),
            pltpu.VMEM((Y - 1, 2, piece, width), BF16),
            pltpu.VMEM((2, piece, width), F32),
            dma((7,)), dma((Y, 2)), dma((Y, 2)), dma((Y - 1, 2)), dma((Y - 1, 2)),
            dma((4, 2, half)), dma((4, 2, half)), dma((M - 1,)), dma((M - 1,)), dma((2,)), dma((2,)),
            dma((M,)), dma((Y, 2)), dma((Y, 2)), dma((Y - 1, 2)), dma((Y - 1, 2)),
        ],
        compiler_params=pltpu.CompilerParams(
            collective_id=0, has_side_effects=True, vmem_limit_bytes=60 * 2 ** 20),
        cost_estimate=pl.CostEstimate(flops=flops, bytes_accessed=32 * 2 ** 20, transcendentals=0),
        name="layer",
    )(
        request_adapter, adapter_row_index, request_token_length, continues_previous,
        request_cache_block, cached_length,
        stream, prenorm_gain.reshape(1, M * width), freq[None, :],
        query_weight.reshape(M, width, nq), key_weight.reshape(M, width, nk),
        value_weight.reshape(M, width, nk), wo, adapter_down_rows, adapter_up_query,
        cached_rotated_keys, cached_value_rows,
    )


def solution(mesh):
    placed = (
        P("group", "mp"), P(), P(None, "mp"), P(None, "mp"), P(None, "mp"), P("mp", None),
        P("group", None, "mp"), P("group", None, "mp"), P(), P(), P(), P(), P(), P(),
        P("group", None, "mp"), P("group", None, "mp"),
    )
    return jax.shard_map(
        functools.partial(on_device, mesh.shape["group"], mesh.shape["mp"]),
        mesh=mesh, in_specs=placed, out_specs=P("group", "mp"), check_vma=False,
    )
```
